32 devices in a mesh: dp: 8 (over z, x), fsdp: 4 (over y, core).
Axes of the slice: x: 2, y: 2, z: 4, core: 2. Of those that a mesh axis runs over, the one named last changes fastest.
Arguments:
- tokens: bfloat16 [16384, 576], P(('dp', 'fsdp')), may hold values from -6 to 6
- seg_ids: int32 [16384], P(('dp', 'fsdp')), may hold values from -1 to 7, as said below
- gains: bfloat16 [576, 2], P('dp'), may hold values from 0.5 to 1.5
- wqkv: bfloat16 [576, 960], P('dp', 'fsdp'), may hold values from -0.25 to 0.25
- w_out: bfloat16 [576, 576], P('dp', 'fsdp'), may hold values from -1 to 1
- w_gate: bfloat16 [576, 1536], P('dp', 'fsdp'), may hold values from -0.25 to 0.25
- w_up: bfloat16 [576, 1536], P('dp', 'fsdp'), may hold values from -0.25 to 0.25
- w_down: bfloat16 [1536, 576], P('dp', 'fsdp'), may hold values from -0.15625 to 0.15625
- cotangent: bfloat16 [16384, 576], P(('dp', 'fsdp')), may hold values from -6 to 6
Outputs:
- out_tokens: bfloat16 [16384, 576], P(('dp', 'fsdp'))
- grad_tokens: bfloat16 [16384, 576], P(('dp', 'fsdp'))
- grad_gains: float32 [576, 2], P('dp')
- grad_wqkv: float32 [576, 960], P('dp', 'fsdp')
- grad_w_out: float32 [576, 576], P('dp', 'fsdp')
- grad_w_gate: float32 [576, 1536], P('dp', 'fsdp')
- grad_w_up: float32 [576, 1536], P('dp', 'fsdp')
- grad_w_down: float32 [1536, 576], P('dp', 'fsdp')
The draws below stay inside these ranges and needn't reach their ends.
Inputs may be any that keep to these rules, and one draw needn't show every extreme that they name: `seg_ids`: within each device's 512 slots the live slots come first and carry segment numbers starting at 0 that never fall and rise by one at each new segment, at most 8 segments on a device; the other slots hold -1. One device is filled by a single segment of 512 tokens, and another is filled by 8 segments of 64 tokens.
All inputs are finite; a program needn't handle non-finite values.
Results may differ from the reference program's by a relative error of at most 0.014.
Values may be sent and summed in bfloat16 or wider, within the bound.
A program may use at most 128 MiB of HBM per device.

```python
import jax
import jax.numpy as jnp
from jax import lax

D = 576
HEADS = 9
KV_HEADS = 3
HEAD = 64
FF = 1536
TOK_DEV = 512
TOKENS = 16384


def draw_seg_ids(key, part):
    key = jax.random.fold_in(key, 11)
    blocks = TOKENS // TOK_DEV
    key_live, key_start = jax.random.split(key)
    live_count = jax.random.randint(key_live, (blocks, 1), TOK_DEV // 2, TOK_DEV + 1)
    live_count = live_count.at[0, 0].set(TOK_DEV)
    live_count = live_count.at[1, 0].set(TOK_DEV)
    starting = jax.random.randint(key_start, (blocks, TOK_DEV), 0, max(TOK_DEV // 4, 2)) == 0
    slot_ids = jnp.arange(TOK_DEV, dtype=jnp.int32)[None, :]
    starting = starting & (slot_ids > 0)
    starting = starting.at[0].set(False)
    even_starts = (slot_ids[0] % (TOK_DEV // 8) == 0) & (slot_ids[0] > 0)
    starting = starting.at[1].set(even_starts)
    segment = jnp.minimum(jnp.cumsum(starting.astype(jnp.int32), axis=1), 7)
    segment = jnp.where(slot_ids < live_count, segment, -1)
    return segment.reshape(-1).astype(jnp.int32)


def with_spikes(values, rng, source, target, parts, factor):
    def block_of(dim):
        return (jnp.arange(values.shape[dim]) // (values.shape[dim] // parts)).reshape((-1,) + (1,) * (values.ndim - 1 - dim))

    one_side = jax.random.permutation(rng, parts)[block_of(target)]
    other_side = (block_of(target) + parts // 2) % parts
    return jnp.where((block_of(source) == one_side) | (block_of(source) == other_side), factor * values, values)


def block_levels(key, extent, shards, smallest, top_value):
    level = 1.0
    for dim, parts in shards:
        steps = jax.random.uniform(jax.random.fold_in(jax.random.fold_in(key, 6), dim), (parts,), jnp.float32, smallest / len(shards), top_value / len(shards))
        level = level * jnp.repeat(jnp.exp(steps), extent[dim] // parts).reshape((-1,) + (1,) * (len(extent) - 1 - dim))
    return level


def centred(rng, dims, spread, limit, shards=(), kind=jnp.bfloat16):
    values = spread * jax.random.normal(rng, dims, jnp.float32)
    if shards:
        values = values * block_levels(rng, dims, shards, -0.22, 0.18)
    return jnp.clip(values, -limit, limit).astype(kind)


def bell_draw_with(own_key, extent, deviation, limit, cuts, heavy, kind=jnp.bfloat16):
    entries = deviation * jax.random.normal(own_key, extent, jnp.float32)
    if cuts:
        entries = entries * block_levels(own_key, extent, cuts, -0.22, 0.18)
    return jnp.clip(with_spikes(entries, jax.random.fold_in(own_key, 3), *heavy), -limit, limit).astype(kind)


def setup_inputs(seed: int = 0) -> dict:
    arg_keys = jax.random.split(jax.random.key(seed), 10)
    tokens = centred(arg_keys[0], (TOKENS, D), 1.0, 6.0, ((0, 32),))
    seg_ids = draw_seg_ids(jax.random.fold_in(arg_keys[9], 71), 0)
    gains = jnp.clip(1.0 + 0.1 * jax.random.normal(arg_keys[2], (D, 2), jnp.float32), 0.5, 1.5).astype(jnp.bfloat16)
    wqkv = centred(arg_keys[3], (D, (HEADS + 2 * KV_HEADS) * HEAD), D ** -0.5, 0.25, ((0, 8), (1, 4)))
    w_out = centred(arg_keys[4], (HEADS * HEAD, D), (HEADS * HEAD // 16) ** -0.5, 1.0, ((0, 8), (1, 4)))
    w_gate = centred(arg_keys[5], (D, FF), D ** -0.5, 0.25, ((0, 8), (1, 4)))
    w_up = centred(arg_keys[6], (D, FF), D ** -0.5, 0.25, ((0, 8), (1, 4)))
    w_down = centred(arg_keys[7], (FF, D), FF ** -0.5, 0.15625, ((0, 8), (1, 4)))
    cotangent = bell_draw_with(arg_keys[8], (TOKENS, D), 1.0, 6.0, ((0, 32),), (0, 1, 32, 2.75))
    return {"tokens": tokens, "seg_ids": seg_ids, "gains": gains, "wqkv": wqkv, "w_out": w_out, "w_gate": w_gate, "w_up": w_up, "w_down": w_down, "cotangent": cotangent}


highest = lax.Precision.HIGHEST
epsilon = 1e-05
rope_base = 100000.0
masked_score = -1000000000.0

@jax.custom_vjp
def low(v):
    return lax.optimization_barrier(v.astype(jnp.bfloat16)).astype(jnp.float32)

@jax.custom_vjp
def low_back(v):
    return v

def low_keep(v):
    return (low(v), None)

def low_pass(kept, grad):
    return (grad,)

def back_keep(v):
    return (v, None)

def back_low(kept, grad):
    return (low(grad),)
low.defvjp(low_keep, low_pass)
low_back.defvjp(back_keep, back_low)

def turned(values_in):
    half_size = values_in.shape[-1] // 2
    return jnp.concatenate([-values_in[..., half_size:], values_in[..., :half_size]], axis=-1)

def rotate(values_in, cosine, sine):
    return values_in * cosine + turned(values_in) * sine

def tables(seg_ids, head_size):
    count_rows = seg_ids.shape[0]
    slot_ids = jnp.arange(count_rows, dtype=jnp.int32)
    matching = seg_ids[:, None] == seg_ids[None, :]
    first_slot = lax.optimization_barrier(jnp.min(jnp.where(matching, slot_ids[None, :], count_rows), axis=1)).astype(jnp.int32)
    position = (slot_ids - first_slot).astype(jnp.float32)
    frequency = rope_base ** (-jnp.arange(0, head_size, 2, dtype=jnp.float32) / head_size)
    angles = position[:, None] * frequency[None, :]
    angles = jnp.concatenate([angles, angles], axis=1)
    causal = slot_ids[None, :] <= slot_ids[:, None]
    allowed = matching & causal & (seg_ids >= 0)[None, :] | (slot_ids[None, :] == slot_ids[:, None])
    return (jnp.cos(angles), jnp.sin(angles), allowed)

def block_forward(weights, inputs_f, seg_ids):
    gains_f, wqkv_f, w_out_f, w_gate_f, w_up_f, w_down_f = weights
    rows_count = inputs_f.shape[0]
    group_size = HEADS // KV_HEADS
    width_q = HEADS * HEAD
    width_k = KV_HEADS * HEAD
    cosine, sine, allowed = tables(seg_ids, HEAD)
    live_rows = (seg_ids >= 0)[:, None]
    scale_one = lax.rsqrt(lax.optimization_barrier(jnp.mean(inputs_f * inputs_f, axis=1, keepdims=True)) + epsilon)
    normed = low(inputs_f * scale_one * gains_f[:, 0])
    projected = low_back(jnp.dot(normed, wqkv_f, precision=highest))
    queries = projected[:, :width_q].reshape(rows_count, HEADS, HEAD)
    keys_raw = projected[:, width_q:width_q + width_k].reshape(rows_count, KV_HEADS, HEAD)
    values_raw = projected[:, width_q + width_k:].reshape(rows_count, KV_HEADS, HEAD)
    queries = low(rotate(queries, cosine[:, None, :], sine[:, None, :]))
    keys_low = low(rotate(keys_raw, cosine[:, None, :], sine[:, None, :]))
    values_low = low(values_raw)
    grouped = queries.reshape(rows_count, KV_HEADS, group_size, HEAD)
    scores = jnp.einsum('qgmd,kgd->gmqk', grouped, keys_low, precision=highest) * HEAD ** (-0.5)
    scores = low_back(scores)
    scores = jnp.where(allowed[None, None], scores, masked_score)
    highest_score = lax.optimization_barrier(jnp.max(scores, axis=-1, keepdims=True))
    weights_exp = jnp.exp(scores - highest_score)
    prob_low = low(weights_exp / lax.optimization_barrier(jnp.sum(weights_exp, axis=-1, keepdims=True)))
    mixed = jnp.einsum('gmqk,kgd->qgmd', prob_low, values_low, precision=highest).reshape(rows_count, width_q)
    attended = low(low_back(mixed))
    middle = inputs_f + low_back(jnp.dot(attended, w_out_f, precision=highest))
    scale_two = lax.rsqrt(lax.optimization_barrier(jnp.mean(middle * middle, axis=1, keepdims=True)) + epsilon)
    normed_two = low(middle * scale_two * gains_f[:, 1])
    gate_pre = low_back(jnp.dot(normed_two, w_gate_f, precision=highest))
    up_pre = low_back(jnp.dot(normed_two, w_up_f, precision=highest))
    hidden = low(gate_pre * jax.nn.sigmoid(gate_pre) * up_pre)
    result = middle + low_back(jnp.dot(hidden, w_down_f, precision=highest))
    return jnp.where(live_rows, result, 0.0)

def reference(tokens, seg_ids, gains, wqkv, w_out, w_gate, w_up, w_down, cotangent):
    blocks = TOKENS // TOK_DEV
    seg_blocks = seg_ids.reshape(blocks, TOK_DEV)

    def whole(inputs_f, gains_f, wqkv_f, w_out_f, w_gate_f, w_up_f, w_down_f):
        weights = (gains_f, wqkv_f, w_out_f, w_gate_f, w_up_f, w_down_f)

        def one_block(pair):
            return block_forward(weights, pair[0], pair[1])
        outputs = lax.map(jax.checkpoint(one_block), (inputs_f.reshape(blocks, TOK_DEV, D), seg_blocks))
        return outputs.reshape(TOKENS, D)
    primals = (tokens.astype(jnp.float32), gains.astype(jnp.float32), wqkv.astype(jnp.float32), w_out.astype(jnp.float32), w_gate.astype(jnp.float32), w_up.astype(jnp.float32), w_down.astype(jnp.float32))
    result, pullback = jax.vjp(whole, *primals)
    grads = pullback(cotangent.astype(jnp.float32))
    return (result.astype(jnp.bfloat16), grads[0].astype(jnp.bfloat16), grads[1], grads[2], grads[3], grads[4], grads[5], grads[6])
```

```python
import functools

import jax
import jax.numpy as jnp
from jax import lax
from jax.experimental import pallas as pl
from jax.experimental.pallas import tpu as pltpu
from jax.sharding import PartitionSpec as P

HEADS = 9
KV_HEADS = 3
HEAD = 64
MESH = pl.DeviceIdType.MESH
WIDE = 384


epsilon = 1e-05
rope_base = 100000.0
masked_score = -1000000000.0


def position():
    d, f = lax.axis_index("dp"), lax.axis_index("fsdp")
    return d // 2, d % 2, f // 2, f % 2


def device(zz, xx, yy, cc):
    return (zz * 2 + xx, yy * 2 + cc)


def columns(yy, cc):
    return pl.ds(pl.multiple_of((yy * 2 + cc) * WIDE, 128), WIDE)


def placed_by(p, first, second):
    return (first, second) if p == 0 else (second, first)


def greet(depth, z, x, y, c):
    barrier = pltpu.get_barrier_semaphore()
    for peer in ((z, 1 - x, y, c), (z, x, 1 - y, c), (z, x, y, 1 - c)):
        pl.semaphore_signal(barrier, inc=1, device_id=device(*peer), device_id_type=MESH)

    def call(k, carry):
        pl.semaphore_signal(
            barrier, inc=1, device_id=device((z + k) % depth, x, y, c), device_id_type=MESH
        )
        return carry

    lax.fori_loop(1, depth, call, 0)
    pl.semaphore_wait(barrier, depth + 2)


def remote(src, dst, send_sem, recv_sem, peer):
    return pltpu.make_async_remote_copy(
        src_ref=src,
        dst_ref=dst,
        send_sem=send_sem,
        recv_sem=recv_sem,
        device_id=device(*peer),
        device_id_type=MESH,
    )


def gather_kernel(
    depth, w_ref, g_ref, o_ref, go_ref,
    own_sem, got, sent_z, sent_a, sent_b, sent_c, g_own, g_got, g_sent_z, g_sent_x,
):
    z, x, y, c = position()
    mine = ((x, y), (y, x))
    peers_a = ((z, 1 - x, y, c), (z, x, 1 - y, c))
    peers_b = ((z, x, 1 - y, c), (z, 1 - x, y, c))
    core = (z, x, y, 1 - c)
    greet(depth, z, x, y, c)

    def slot(p, zz, a, b, cc):
        xx, yy = placed_by(p, a, b)
        return o_ref.at[p, zz * 2 + xx, :, columns(yy, cc)]

    def arrive(p, zz, a, b, cc):
        return got.at[p, zz, a * 4 + b * 2 + cc]

    def copy(p, zz, a, b, cc, send_sem, peer, src=None):
        dst = slot(p, zz, a, b, cc)
        return remote(dst if src is None else src, dst, send_sem, arrive(p, zz, a, b, cc), peer)

    def to_a(p, zz, a, b, src=None):
        return copy(p, zz, a, b, c, sent_a.at[p, zz], peers_a[p], src)

    def to_b(p, zz, a, b, src=None):
        return copy(p, zz, a, b, c, sent_b.at[p, zz, a], peers_b[p], src)

    def to_core(p, zz, a, b, src=None):
        return copy(p, zz, a, b, c, sent_c.at[p, zz, a * 2 + b], core, src)

    def to_z(p, zz, src):
        a, b = mine[p]
        return copy(p, z, a, b, c, sent_z.at[p, zz], (zz, x, y, c), src)

    def received(p, zz, a, b, cc):
        copy(p, zz, a, b, cc, sent_a.at[p, zz], core).wait_recv()

    def gain_copy(zz, xx, send_sem, peer, src=None):
        dst = go_ref.at[zz * 2 + xx]
        return remote(dst if src is None else src, dst, send_sem, g_got.at[zz, xx], peer)

    x_peer = peers_a[0]
    local = [
        pltpu.make_async_copy(w_ref.at[p], slot(p, z, *mine[p], c), own_sem.at[p]) for p in (0, 1)
    ] + [pltpu.make_async_copy(g_ref, go_ref.at[z * 2 + x], g_own)]
    for p in (0, 1):
        to_a(p, z, *mine[p], w_ref.at[p]).start()
    gain_copy(z, x, g_sent_x.at[z], x_peer, g_ref).start()

    def send_z(k, carry):
        zz = (z + k) % depth
        for p in (0, 1):
            to_z(p, zz, w_ref.at[p]).start()
        gain_copy(z, x, g_sent_z.at[zz], (zz, x, y, c), g_ref).start()
        return carry

    lax.fori_loop(1, depth, send_z, 0)
    for p in (0, 1):
        to_b(p, z, *mine[p], w_ref.at[p]).start()
        to_core(p, z, *mine[p], w_ref.at[p]).start()
    for one in local:
        one.start()

    def second(zz):
        for p in (0, 1):
            a, b = mine[p]
            received(p, zz, 1 - a, b, c)
            to_b(p, zz, 1 - a, b).start()
            to_core(p, zz, 1 - a, b).start()

    def pass_on(k, carry):
        zz = (z + k) % depth
        for p in (0, 1):
            a, b = mine[p]
            received(p, zz, a, b, c)
            to_a(p, zz, a, b).start()
            to_b(p, zz, a, b).start()
            to_core(p, zz, a, b).start()
        gain_copy(zz, x, g_sent_z.at[zz], x_peer).wait_recv()
        gain_copy(zz, x, g_sent_x.at[zz], x_peer).start()
        second((z + k - 1) % depth)
        return carry

    lax.fori_loop(1, depth, pass_on, 0)
    second((z + depth - 1) % depth)

    def third(k, carry):
        zz = (z + k) % depth
        for p in (0, 1):
            b = mine[p][1]
            for a in (0, 1):
                received(p, zz, a, 1 - b, c)
                to_core(p, zz, a, 1 - b).start()
        return carry

    lax.fori_loop(0, depth, third, 0)

    def finish(k, carry):
        zz = (z + k) % depth
        for p in (0, 1):
            a_own, b_own = mine[p]
            for a in (0, 1):
                for b in (0, 1):
                    received(p, zz, a, b, 1 - c)
                    to_core(p, zz, a, b).wait_send()
                to_b(p, zz, a, b_own).wait_send()
            to_a(p, zz, a_own, b_own).wait_send()
        gain_copy(zz, 1 - x, g_sent_x.at[zz], x_peer).wait_recv()
        gain_copy(zz, x, g_sent_x.at[zz], x_peer).wait_send()
        return carry

    lax.fori_loop(0, depth, finish, 0)

    def finish_z(k, carry):
        zz = (z + k) % depth
        for p in (0, 1):
            to_z(p, zz, w_ref.at[p]).wait_send()
        gain_copy(z, x, g_sent_z.at[zz], (zz, x, y, c), g_ref).wait_send()
        return carry

    lax.fori_loop(1, depth, finish_z, 0)
    for one in local:
        one.wait()


def gather_all(packed, gains_packed):
    n = lax.axis_size("dp")
    depth, rows = n // 2, packed.shape[1]
    dma = pltpu.SemaphoreType.DMA
    return pl.pallas_call(
        functools.partial(gather_kernel, depth),
        out_shape=(
            jax.ShapeDtypeStruct((2, n, rows, 4 * WIDE), packed.dtype),
            jax.ShapeDtypeStruct((n, *gains_packed.shape), gains_packed.dtype),
        ),
        in_specs=[pl.BlockSpec(memory_space=pl.ANY)] * 2,
        out_specs=(pl.BlockSpec(memory_space=pl.ANY),) * 2,
        scratch_shapes=[
            dma((2,)), dma((2, depth, 8)), dma((2, depth)), dma((2, depth)),
            dma((2, depth, 2)), dma((2, depth, 4)),
            dma, dma((depth, 2)), dma((depth,)), dma((depth,)),
        ],
        compiler_params=pltpu.CompilerParams(collective_id=1, has_side_effects=True),
    )(packed, gains_packed)


def reduce_kernel(
    depth, w_ref, g_ref, o_ref, go_ref,
    from_core, from_first, from_second, from_z, g_in, g_sum, g_z,
    c_sent, c_got, a_sent, a_got, b_sent, b_got, z_sent, z_got,
    g_sent, g_got, gz_sent, gz_got,
):
    z, x, y, c = position()
    mine = ((y, x), (x, y))
    peers_a = ((z, x, 1 - y, c), (z, 1 - x, y, c))
    peers_b = ((z, 1 - x, y, c), (z, x, 1 - y, c))
    core = (z, x, y, 1 - c)
    greet(depth, z, x, y, c)

    def block(p, zz, a, b, cc):
        yy, xx = placed_by(p, a, b)
        return w_ref.at[p, zz * 2 + xx, :, columns(yy, cc)]

    def core_copy(p, zz, a, b):
        at = (p, zz, a * 2 + b)
        return remote(block(p, zz, a, b, 1 - c), from_core.at[at], c_sent.at[at], c_got.at[at], core)

    def a_copy(p, zz, a, b):
        at = (p, zz, b)
        return remote(
            from_core.at[p, zz, a * 2 + b], from_first.at[at], a_sent.at[at], a_got.at[at], peers_a[p]
        )

    def b_copy(p, zz, b):
        return remote(
            from_first.at[p, zz, b], from_second.at[p, zz], b_sent.at[p, zz], b_got.at[p, zz], peers_b[p]
        )

    def z_copy(p, zz):
        return remote(
            from_second.at[p, zz], from_z.at[p, z], z_sent.at[p, zz], z_got.at[p, z], (zz, x, y, c)
        )

    def z_from(p, zz):
        return remote(
            from_second.at[p, zz], from_z.at[p, zz], z_sent.at[p, zz], z_got.at[p, zz], (zz, x, y, c)
        )

    def wide(ref):
        return ref[...].astype(jnp.float32)

    def g_copy(step, peer):
        src = g_ref if step == 0 else g_sum.at[step - 1]
        return remote(src, g_in.at[step], g_sent.at[step], g_got.at[step], peer)

    def gz_copy(zz):
        return remote(
            g_sum.at[2, zz * 2 + x], g_z.at[z], gz_sent.at[zz], gz_got.at[z], (zz, x, y, c)
        )

    def gz_from(zz):
        return remote(
            g_sum.at[2, zz * 2 + x], g_z.at[zz], gz_sent.at[zz], gz_got.at[zz], (zz, x, y, c)
        )

    g_peers = (core, (z, x, 1 - y, c), (z, 1 - x, y, c))

    def add_gains(step):
        g_copy(step, g_peers[step]).wait_recv()
        before = g_ref if step == 0 else g_sum.at[step - 1]
        g_sum[step] = before[...] + g_in[step]

    g_copy(0, g_peers[0]).start()

    for far in (True, False):
        def start_core(k, carry, far=far):
            zz = (z + k) % depth
            for p in (0, 1):
                a, b = mine[p]
                a = 1 - a if far else a
                core_copy(p, zz, a, 1 - b).start()
                core_copy(p, zz, a, b).start()
            return carry

        lax.fori_loop(1, depth + 1, start_core, 0)

    add_gains(0)
    g_copy(1, g_peers[1]).start()

    def first_step(k, carry):
        zz = (z + k) % depth
        for far in (True, False):
            for p in (0, 1):
                a, b = mine[p]
                a = 1 - a
                b = 1 - b if far else b
                core_copy(p, zz, a, b).wait_recv()
                held = from_core.at[p, zz, a * 2 + b]
                held[...] = (wide(held) + wide(block(p, zz, a, b, c))).astype(held.dtype)
                a_copy(p, zz, a, b).start()
        return carry

    lax.fori_loop(1, depth + 1, first_step, 0)
    add_gains(1)
    g_copy(2, g_peers[2]).start()

    def chain(p, zz, b):
        a = mine[p][0]
        core_copy(p, zz, a, b).wait_recv()
        a_copy(p, zz, a, b).wait_recv()
        return (
            wide(block(p, zz, a, b, c))
            + wide(from_core.at[p, zz, a * 2 + b])
            + wide(from_first.at[p, zz, b])
        )

    def second_step(k, carry):
        zz = (z + k) % depth
        for p in (0, 1):
            b = 1 - mine[p][1]
            from_first[p, zz, b] = chain(p, zz, b).astype(from_first.dtype)
            b_copy(p, zz, b).start()
        return carry

    lax.fori_loop(1, depth + 1, second_step, 0)
    add_gains(2)

    def last_sum(p, zz):
        b = mine[p][1]
        total = chain(p, zz, b)
        b_copy(p, zz, b).wait_recv()
        return total + wide(from_second.at[p, zz])

    def third_step(k, carry):
        zz = (z + k) % depth
        for p in (0, 1):
            from_second[p, zz] = last_sum(p, zz).astype(from_second.dtype)
            z_copy(p, zz).start()
        gz_copy(zz).start()
        return carry

    lax.fori_loop(1, depth, third_step, 0)
    for p in (0, 1):
        o_ref[p] = last_sum(p, z)
    go_ref[...] = g_sum[2, z * 2 + x]

    def collect(k, carry):
        zz = (z + k) % depth
        for p in (0, 1):
            z_from(p, zz).wait_recv()
            o_ref[p] += wide(from_z.at[p, zz])
        gz_from(zz).wait_recv()
        go_ref[...] += g_z[zz]
        for p in (0, 1):
            z_copy(p, zz).wait_send()
        gz_copy(zz).wait_send()
        return carry

    lax.fori_loop(1, depth, collect, 0)

    def finish(k, carry):
        zz = (z + k) % depth
        for p in (0, 1):
            a_own, b_own = mine[p]
            for b in (0, 1):
                for a in (0, 1):
                    core_copy(p, zz, a, b).wait_send()
                a_copy(p, zz, 1 - a_own, b).wait_send()
            b_copy(p, zz, 1 - b_own).wait_send()
        return carry

    lax.fori_loop(0, depth, finish, 0)
    for step in range(3):
        g_copy(step, g_peers[step]).wait_send()


def reduce_all(packed, gains_packed):
    n = lax.axis_size("dp")
    depth, rows = n // 2, packed.shape[2]
    dma = pltpu.SemaphoreType.DMA
    low = packed.dtype
    gain_shape = gains_packed.shape[1:]
    vmem = pl.BlockSpec(memory_space=pltpu.VMEM)
    return pl.pallas_call(
        functools.partial(reduce_kernel, depth),
        out_shape=(
            jax.ShapeDtypeStruct((2, rows, WIDE), jnp.float32),
            jax.ShapeDtypeStruct(gain_shape, jnp.float32),
        ),
        in_specs=[vmem] * 2,
        out_specs=(vmem,) * 2,
        scratch_shapes=[
            pltpu.VMEM((2, depth, 4, rows, WIDE), low),
            pltpu.VMEM((2, depth, 2, rows, WIDE), low),
            pltpu.VMEM((2, depth, rows, WIDE), low),
            pltpu.VMEM((2, depth, rows, WIDE), low),
            pltpu.VMEM((3, n, *gain_shape), jnp.float32),
            pltpu.VMEM((3, n, *gain_shape), jnp.float32),
            pltpu.VMEM((depth, *gain_shape), jnp.float32),
            dma((2, depth, 4)), dma((2, depth, 4)),
            dma((2, depth, 2)), dma((2, depth, 2)),
            dma((2, depth)), dma((2, depth)), dma((2, depth)), dma((2, depth)),
            dma((3,)), dma((3,)), dma((depth,)), dma((depth,)),
        ],
        compiler_params=pltpu.CompilerParams(
            collective_id=2, has_side_effects=True, vmem_limit_bytes=40 * 2**20
        ),
    )(packed, gains_packed)


def pack_down(down, blocks, parts):
    rows = down.shape[0] // blocks
    cut = down.reshape(blocks, rows, parts, 144)
    tail = cut[..., 128:].reshape(blocks, 8, rows // 8, parts, 16)
    tail = tail.transpose(0, 2, 3, 1, 4).reshape(blocks, rows // 8, parts, 128)
    tall = jnp.concatenate([cut[..., :128], tail], axis=1)
    tall = tall.reshape(blocks, 3, -1, parts, 128).transpose(0, 2, 3, 1, 4)
    return tall.reshape(blocks, -1, parts, WIDE)


def unpack_down(held):
    blocks, short, parts, _ = held.shape
    tall = held.reshape(blocks, short, parts, 3, 128).transpose(0, 3, 1, 2, 4)
    tall = tall.reshape(blocks, 3 * short, parts, 128)
    rows = short * 8 // 3
    tail = tall[:, rows:].reshape(blocks, rows // 8, parts, 8, 16)
    tail = tail.transpose(0, 3, 1, 2, 4).reshape(blocks, rows, parts, 16)
    return jnp.concatenate([tall[:, :rows], tail], axis=-1).reshape(blocks * rows, parts * 144)


def pack(qkv, out, gate, up, down, blocks, parts):
    def cut(a):
        return a.reshape(blocks, a.shape[0] // blocks, parts, -1)

    pair = jnp.concatenate([cut(qkv), cut(out)], axis=-1)
    short = pair.shape[1]
    rows = -(-2 * short // 16) * 16
    pieces = []
    for top, bottom in ((pair, pack_down(down, blocks, parts)), (cut(gate), cut(up))):
        both = jnp.concatenate(
            [a.astype(jnp.bfloat16).reshape(blocks, short, -1) for a in (top, bottom)], axis=1
        )
        pieces.append(jnp.pad(both, ((0, 0), (0, rows - 2 * short), (0, 0))))
    return jnp.stack(pieces)


def unpack(held, short):
    _, blocks, _, width = held.shape
    parts = width // WIDE
    pair = held[0, :, :short].reshape(blocks * short, parts, WIDE)
    down = unpack_down(held[0, :, short : 2 * short].reshape(blocks, short, parts, WIDE))
    return (
        pair[..., :240].reshape(blocks * short, -1),
        pair[..., 240:].reshape(blocks * short, -1),
        held[1, :, :short].reshape(blocks * short, width),
        held[1, :, short : 2 * short].reshape(blocks * short, width),
        down,
    )


def turned(values_in):
    half_size = values_in.shape[-1] // 2
    return jnp.concatenate([-values_in[..., half_size:], values_in[..., :half_size]], axis=-1)


def rotate(values_in, cosine, sine):
    return values_in * cosine + turned(values_in) * sine


def rotate_back(grads_in, cosine, sine):
    return grads_in * cosine - turned(grads_in * sine)


def tables(seg_ids, head_size):
    count_rows = seg_ids.shape[0]
    slot_ids = jnp.arange(count_rows, dtype=jnp.int32)
    matching = seg_ids[:, None] == seg_ids[None, :]
    first_slot = jnp.min(jnp.where(matching, slot_ids[None, :], count_rows), axis=1)
    position = (slot_ids - first_slot).astype(jnp.float32)
    frequency = rope_base ** (-jnp.arange(0, head_size, 2, dtype=jnp.float32) / head_size)
    angles = position[:, None] * frequency[None, :]
    angles = jnp.concatenate([angles, angles], axis=1)
    causal = slot_ids[None, :] <= slot_ids[:, None]
    allowed = matching & causal & (seg_ids >= 0)[None, :] | (slot_ids[None, :] == slot_ids[:, None])
    return (jnp.cos(angles), jnp.sin(angles), allowed)


def inner_rows(left, right):
    return lax.dot_general(
        left, right, (((0,), (0,)), ((), ())), preferred_element_type=jnp.float32
    )


def times_trans(left, right):
    return lax.dot_general(
        left, right, (((1,), (1,)), ((), ())), preferred_element_type=jnp.float32
    )


def per_device(tokens, seg_ids, gains, wqkv, w_out, w_gate, w_up, w_down, cotangent):
    short = wqkv.shape[0]
    blocks = lax.axis_size("dp")
    spread = jnp.pad(gains.reshape(-1), (0, 2048 - 2 * short)).reshape(16, 128)
    held, held_gains = gather_all(
        pack(wqkv, w_out, w_gate, w_up, w_down, 1, 1)[:, 0], spread
    )
    full_qkv, full_out, full_gate, full_up, full_down = unpack(held, short)
    full_gains = held_gains.reshape(blocks, 2048)[:, : 2 * short].reshape(blocks * short, 2)
    rows_count = tokens.shape[0]
    group_size = HEADS // KV_HEADS
    width_q = HEADS * HEAD
    width_k = KV_HEADS * HEAD
    score_scale = HEAD ** (-0.5)
    cosine, sine, allowed = tables(seg_ids, HEAD)
    cos_heads = cosine[:, None, :]
    sin_heads = sine[:, None, :]
    live_rows = (seg_ids >= 0)[:, None]
    gain_one = full_gains[:, 0].astype(jnp.float32)
    gain_two = full_gains[:, 1].astype(jnp.float32)
    inputs_f = tokens.astype(jnp.float32)
    scale_one = lax.rsqrt(jnp.mean(inputs_f * inputs_f, axis=1, keepdims=True) + epsilon)
    normed = (inputs_f * scale_one * gain_one).astype(jnp.bfloat16)
    projected = jnp.dot(normed, full_qkv, preferred_element_type=jnp.float32)
    queries = rotate(
        projected[:, :width_q].reshape(rows_count, HEADS, HEAD), cos_heads, sin_heads
    ).astype(jnp.bfloat16)
    keys_low = rotate(
        projected[:, width_q : width_q + width_k].reshape(rows_count, KV_HEADS, HEAD),
        cos_heads,
        sin_heads,
    ).astype(jnp.bfloat16)
    values_low = (
        projected[:, width_q + width_k :].reshape(rows_count, KV_HEADS, HEAD).astype(jnp.bfloat16)
    )
    grouped = queries.reshape(rows_count, KV_HEADS, group_size, HEAD)
    outputs_list = []
    totals_list = []
    for head_kv in range(KV_HEADS):
        scores = (
            jnp.einsum(
                "qmd,kd->mqk",
                grouped[:, head_kv],
                keys_low[:, head_kv],
                preferred_element_type=jnp.float32,
            )
            * score_scale
        )
        scores = jnp.where(allowed[None], scores, masked_score)
        highest_score = jnp.max(scores, axis=-1, keepdims=True)
        weights_exp = jnp.exp(scores - highest_score)
        total_weight = jnp.sum(weights_exp, axis=-1, keepdims=True)
        prob_low = (weights_exp / total_weight).astype(jnp.bfloat16)
        outputs_list.append(
            jnp.einsum(
                "mqk,kd->qmd", prob_low, values_low[:, head_kv], preferred_element_type=jnp.float32
            )
        )
        totals_list.append(highest_score + jnp.log(total_weight))
    attended = jnp.stack(outputs_list, axis=1).reshape(rows_count, width_q).astype(jnp.bfloat16)
    middle = inputs_f + jnp.dot(attended, full_out, preferred_element_type=jnp.float32)
    scale_two = lax.rsqrt(jnp.mean(middle * middle, axis=1, keepdims=True) + epsilon)
    normed_two = (middle * scale_two * gain_two).astype(jnp.bfloat16)
    gate_pre = jnp.dot(normed_two, full_gate, preferred_element_type=jnp.float32)
    up_pre = jnp.dot(normed_two, full_up, preferred_element_type=jnp.float32)
    sigmoid_gate = jax.nn.sigmoid(gate_pre)
    activated = gate_pre * sigmoid_gate
    hidden = (activated * up_pre).astype(jnp.bfloat16)
    result = middle + jnp.dot(hidden, full_down, preferred_element_type=jnp.float32)
    out_tokens = jnp.where(live_rows, result, 0.0).astype(jnp.bfloat16)
    grad_out = jnp.where(live_rows, cotangent, jnp.zeros_like(cotangent))
    grad_down = inner_rows(hidden, grad_out)
    grad_hidden = times_trans(grad_out, full_down)
    grad_gate_pre = (
        grad_hidden * up_pre * sigmoid_gate * (1.0 + gate_pre * (1.0 - sigmoid_gate))
    ).astype(jnp.bfloat16)
    grad_up_pre = (grad_hidden * activated).astype(jnp.bfloat16)
    grad_gate = inner_rows(normed_two, grad_gate_pre)
    grad_up = inner_rows(normed_two, grad_up_pre)
    grad_normed_two = times_trans(grad_gate_pre, full_gate) + times_trans(grad_up_pre, full_up)
    grad_gain_two = jnp.sum(grad_normed_two * middle * scale_two, axis=0)
    weighted_two = grad_normed_two * gain_two
    grad_middle = (
        grad_out.astype(jnp.float32)
        + scale_two * weighted_two
        - middle * scale_two**3 * jnp.mean(weighted_two * middle, axis=1, keepdims=True)
    )
    grad_branch = grad_middle.astype(jnp.bfloat16)
    grad_wout = inner_rows(attended, grad_branch)
    grad_attended = (
        times_trans(grad_branch, full_out)
        .astype(jnp.bfloat16)
        .reshape(rows_count, KV_HEADS, group_size, HEAD)
    )
    query_grads = []
    key_grads = []
    value_grads = []
    for head_kv in range(KV_HEADS):
        query_part = grouped[:, head_kv]
        key_part = keys_low[:, head_kv]
        value_part = values_low[:, head_kv]
        grad_part = grad_attended[:, head_kv]
        scores = (
            jnp.einsum("qmd,kd->mqk", query_part, key_part, preferred_element_type=jnp.float32)
            * score_scale
        )
        scores = jnp.where(allowed[None], scores, masked_score)
        probs_full = jnp.exp(scores - totals_list[head_kv])
        prob_low = probs_full.astype(jnp.bfloat16)
        value_grads.append(
            jnp.einsum("mqk,qmd->kd", prob_low, grad_part, preferred_element_type=jnp.float32)
        )
        grad_prob = jnp.einsum(
            "qmd,kd->mqk", grad_part, value_part, preferred_element_type=jnp.float32
        )
        row_delta = jnp.sum(grad_prob * probs_full, axis=-1, keepdims=True)
        grad_scores = (probs_full * (grad_prob - row_delta)).astype(jnp.bfloat16)
        query_grads.append(
            jnp.einsum("mqk,kd->qmd", grad_scores, key_part, preferred_element_type=jnp.float32)
            * score_scale
        )
        key_grads.append(
            jnp.einsum("mqk,qmd->kd", grad_scores, query_part, preferred_element_type=jnp.float32)
            * score_scale
        )
    grad_queries = rotate_back(
        jnp.stack(query_grads, axis=1).reshape(rows_count, HEADS, HEAD), cos_heads, sin_heads
    )
    grad_keys = rotate_back(jnp.stack(key_grads, axis=1), cos_heads, sin_heads)
    grad_values = jnp.stack(value_grads, axis=1)
    grad_projected = jnp.concatenate(
        [
            grad_queries.reshape(rows_count, width_q),
            grad_keys.reshape(rows_count, width_k),
            grad_values.reshape(rows_count, width_k),
        ],
        axis=1,
    ).astype(jnp.bfloat16)
    grad_qkv = inner_rows(normed, grad_projected)
    grad_normed = times_trans(grad_projected, full_qkv)
    grad_gain_one = jnp.sum(grad_normed * inputs_f * scale_one, axis=0)
    weighted_one = grad_normed * gain_one
    grad_inputs = (
        grad_middle
        + scale_one * weighted_one
        - inputs_f * scale_one**3 * jnp.mean(weighted_one * inputs_f, axis=1, keepdims=True)
    )
    grad_tokens = grad_inputs.astype(jnp.bfloat16)
    grad_gains = jnp.stack([grad_gain_one, grad_gain_two], axis=1)
    packed = pack(grad_qkv, grad_wout, grad_gate, grad_up, grad_down, blocks, lax.axis_size("fsdp"))
    flat_gains = jnp.pad(grad_gains.reshape(blocks, -1), ((0, 0), (0, 1024 - 2 * short)))
    owned, owned_gains = reduce_all(packed, flat_gains.reshape(blocks, 8, 128))
    own_qkv, own_out, own_gate, own_up, own_down = unpack(owned[:, None], short)
    own_gains = owned_gains.reshape(-1)[: 2 * short].reshape(short, 2)
    return (out_tokens, grad_tokens, own_gains, own_qkv, own_out, own_gate, own_up, own_down)


def solution(mesh):
    placed = (
        P(("dp", "fsdp"), None),
        P(("dp", "fsdp")),
        P("dp", None),
        P("dp", "fsdp"),
        P("dp", "fsdp"),
        P("dp", "fsdp"),
        P("dp", "fsdp"),
        P("dp", "fsdp"),
        P(("dp", "fsdp"), None),
    )
    return jax.shard_map(
        per_device,
        mesh=mesh,
        in_specs=placed,
        out_specs=(
            P(("dp", "fsdp"), None),
            P(("dp", "fsdp"), None),
            P("dp", None),
            P("dp", "fsdp"),
            P("dp", "fsdp"),
            P("dp", "fsdp"),
            P("dp", "fsdp"),
            P("dp", "fsdp"),
        ),
        check_vma=False,
    )
```

```python
import functools

import jax
import jax.numpy as jnp
import numpy as np
from jax import lax
from jax.experimental import pallas as pl
from jax.experimental.pallas import tpu as pltpu
from jax.sharding import PartitionSpec as P

HEADS = 9
KV_HEADS = 3
HEAD = 64
MESH = pl.DeviceIdType.MESH
WIDE = 384


epsilon = 1e-05
rope_base = 100000.0
masked_score = -1000000000.0


def position():
    d, f = lax.axis_index("dp"), lax.axis_index("fsdp")
    return d // 2, d % 2, f // 2, f % 2


def device(zz, xx, yy, cc):
    return (zz * 2 + xx, yy * 2 + cc)


def columns(yy, cc):
    return pl.ds(pl.multiple_of((yy * 2 + cc) * WIDE, 128), WIDE)


def placed_by(p, first, second):
    return (first, second) if p == 0 else (second, first)


def greet(depth, z, x, y, c):
    barrier = pltpu.get_barrier_semaphore()
    for peer in ((z, 1 - x, y, c), (z, x, 1 - y, c), (z, x, y, 1 - c)):
        pl.semaphore_signal(barrier, inc=1, device_id=device(*peer), device_id_type=MESH)

    def call(k, carry):
        pl.semaphore_signal(
            barrier, inc=1, device_id=device((z + k) % depth, x, y, c), device_id_type=MESH
        )
        return carry

    lax.fori_loop(1, depth, call, 0)
    pl.semaphore_wait(barrier, depth + 2)


def remote(src, dst, send_sem, recv_sem, peer):
    return pltpu.make_async_remote_copy(
        src_ref=src,
        dst_ref=dst,
        send_sem=send_sem,
        recv_sem=recv_sem,
        device_id=device(*peer),
        device_id_type=MESH,
    )


def gather_kernel(
    depth, w_ref, g_ref, o_ref, go_ref,
    own_sem, got, sent_z, sent_a, sent_b, sent_c, g_own, g_got, g_sent_z, g_sent_x,
):
    z, x, y, c = position()
    mine = ((x, y), (y, x))
    peers_a = ((z, 1 - x, y, c), (z, x, 1 - y, c))
    peers_b = ((z, x, 1 - y, c), (z, 1 - x, y, c))
    core = (z, x, y, 1 - c)
    greet(depth, z, x, y, c)

    def slot(p, zz, a, b, cc):
        xx, yy = placed_by(p, a, b)
        return o_ref.at[p, zz * 2 + xx, :, columns(yy, cc)]

    def arrive(p, zz, a, b, cc):
        return got.at[p, zz, a * 4 + b * 2 + cc]

    def copy(p, zz, a, b, cc, send_sem, peer, src=None):
        dst = slot(p, zz, a, b, cc)
        return remote(dst if src is None else src, dst, send_sem, arrive(p, zz, a, b, cc), peer)

    def to_a(p, zz, a, b, src=None):
        return copy(p, zz, a, b, c, sent_a.at[p, zz], peers_a[p], src)

    def to_b(p, zz, a, b, src=None):
        return copy(p, zz, a, b, c, sent_b.at[p, zz, a], peers_b[p], src)

    def to_core(p, zz, a, b, src=None):
        return copy(p, zz, a, b, c, sent_c.at[p, zz, a * 2 + b], core, src)

    def to_z(p, zz, src):
        a, b = mine[p]
        return copy(p, z, a, b, c, sent_z.at[p, zz], (zz, x, y, c), src)

    def received(p, zz, a, b, cc):
        copy(p, zz, a, b, cc, sent_a.at[p, zz], core).wait_recv()

    def gain_copy(zz, xx, send_sem, peer, src=None):
        dst = go_ref.at[zz * 2 + xx]
        return remote(dst if src is None else src, dst, send_sem, g_got.at[zz, xx], peer)

    x_peer = peers_a[0]
    local = [
        pltpu.make_async_copy(w_ref.at[p], slot(p, z, *mine[p], c), own_sem.at[p]) for p in (0, 1)
    ] + [pltpu.make_async_copy(g_ref, go_ref.at[z * 2 + x], g_own)]
    for p in (0, 1):
        to_a(p, z, *mine[p], w_ref.at[p]).start()
    gain_copy(z, x, g_sent_x.at[z], x_peer, g_ref).start()

    def send_z(k, carry):
        zz = (z + k) % depth
        for p in (0, 1):
            to_z(p, zz, w_ref.at[p]).start()
        gain_copy(z, x, g_sent_z.at[zz], (zz, x, y, c), g_ref).start()
        return carry

    lax.fori_loop(1, depth, send_z, 0)
    for p in (0, 1):
        to_b(p, z, *mine[p], w_ref.at[p]).start()
        to_core(p, z, *mine[p], w_ref.at[p]).start()
    for one in local:
        one.start()

    def second(zz):
        for p in (0, 1):
            a, b = mine[p]
            received(p, zz, 1 - a, b, c)
            to_b(p, zz, 1 - a, b).start()
            to_core(p, zz, 1 - a, b).start()

    def pass_on(k, carry):
        zz = (z + k) % depth
        for p in (0, 1):
            a, b = mine[p]
            received(p, zz, a, b, c)
            to_a(p, zz, a, b).start()
            to_b(p, zz, a, b).start()
            to_core(p, zz, a, b).start()
        gain_copy(zz, x, g_sent_z.at[zz], x_peer).wait_recv()
        gain_copy(zz, x, g_sent_x.at[zz], x_peer).start()
        second((z + k - 1) % depth)
        return carry

    lax.fori_loop(1, depth, pass_on, 0)
    second((z + depth - 1) % depth)

    def third(k, carry):
        zz = (z + k) % depth
        for p in (0, 1):
            b = mine[p][1]
            for a in (0, 1):
                received(p, zz, a, 1 - b, c)
                to_core(p, zz, a, 1 - b).start()
        return carry

    lax.fori_loop(0, depth, third, 0)

    def finish(k, carry):
        zz = (z + k) % depth
        for p in (0, 1):
            a_own, b_own = mine[p]
            for a in (0, 1):
                for b in (0, 1):
                    received(p, zz, a, b, 1 - c)
                    to_core(p, zz, a, b).wait_send()
                to_b(p, zz, a, b_own).wait_send()
            to_a(p, zz, a_own, b_own).wait_send()
        gain_copy(zz, 1 - x, g_sent_x.at[zz], x_peer).wait_recv()
        gain_copy(zz, x, g_sent_x.at[zz], x_peer).wait_send()
        return carry

    lax.fori_loop(0, depth, finish, 0)

    def finish_z(k, carry):
        zz = (z + k) % depth
        for p in (0, 1):
            to_z(p, zz, w_ref.at[p]).wait_send()
        gain_copy(z, x, g_sent_z.at[zz], (zz, x, y, c), g_ref).wait_send()
        return carry

    lax.fori_loop(1, depth, finish_z, 0)
    for one in local:
        one.wait()


def gather_all(packed, gains_packed):
    n = lax.axis_size("dp")
    depth, rows = n // 2, packed.shape[1]
    dma = pltpu.SemaphoreType.DMA
    return pl.pallas_call(
        functools.partial(gather_kernel, depth),
        out_shape=(
            jax.ShapeDtypeStruct((2, n, rows, 4 * WIDE), packed.dtype),
            jax.ShapeDtypeStruct((n, *gains_packed.shape), gains_packed.dtype),
        ),
        in_specs=[pl.BlockSpec(memory_space=pl.ANY)] * 2,
        out_specs=(pl.BlockSpec(memory_space=pl.ANY),) * 2,
        scratch_shapes=[
            dma((2,)), dma((2, depth, 8)), dma((2, depth)), dma((2, depth)),
            dma((2, depth, 2)), dma((2, depth, 4)),
            dma, dma((depth, 2)), dma((depth,)), dma((depth,)),
        ],
        compiler_params=pltpu.CompilerParams(collective_id=1, has_side_effects=True),
    )(packed, gains_packed)


def reduce_kernel(
    depth, w_ref, g_ref, o_ref, go_ref,
    from_core, from_first, from_second, from_z, g_in, g_sum, g_z,
    c_sent, c_got, a_sent, a_got, b_sent, b_got, z_sent, z_got,
    g_sent, g_got, gz_sent, gz_got,
):
    z, x, y, c = position()
    mine = ((y, x), (x, y))
    peers_a = ((z, x, 1 - y, c), (z, 1 - x, y, c))
    peers_b = ((z, 1 - x, y, c), (z, x, 1 - y, c))
    core = (z, x, y, 1 - c)
    greet(depth, z, x, y, c)

    def block(p, zz, a, b, cc):
        yy, xx = placed_by(p, a, b)
        return w_ref.at[p, zz * 2 + xx, :, columns(yy, cc)]

    def core_copy(p, zz, a, b):
        at = (p, zz, a * 2 + b)
        return remote(block(p, zz, a, b, 1 - c), from_core.at[at], c_sent.at[at], c_got.at[at], core)

    def a_copy(p, zz, a, b):
        at = (p, zz, b)
        return remote(
            from_core.at[p, zz, a * 2 + b], from_first.at[at], a_sent.at[at], a_got.at[at], peers_a[p]
        )

    def b_copy(p, zz, b):
        return remote(
            from_first.at[p, zz, b], from_second.at[p, zz], b_sent.at[p, zz], b_got.at[p, zz], peers_b[p]
        )

    def z_copy(p, zz):
        return remote(
            from_second.at[p, zz], from_z.at[p, z], z_sent.at[p, zz], z_got.at[p, z], (zz, x, y, c)
        )

    def z_from(p, zz):
        return remote(
            from_second.at[p, zz], from_z.at[p, zz], z_sent.at[p, zz], z_got.at[p, zz], (zz, x, y, c)
        )

    def wide(ref):
        return ref[...].astype(jnp.float32)

    def g_copy(step, peer):
        src = g_ref if step == 0 else g_sum.at[step - 1]
        return remote(src, g_in.at[step], g_sent.at[step], g_got.at[step], peer)

    def gz_copy(zz):
        return remote(
            g_sum.at[2, zz * 2 + x], g_z.at[z], gz_sent.at[zz], gz_got.at[z], (zz, x, y, c)
        )

    def gz_from(zz):
        return remote(
            g_sum.at[2, zz * 2 + x], g_z.at[zz], gz_sent.at[zz], gz_got.at[zz], (zz, x, y, c)
        )

    g_peers = (core, (z, x, 1 - y, c), (z, 1 - x, y, c))

    def add_gains(step):
        g_copy(step, g_peers[step]).wait_recv()
        before = g_ref if step == 0 else g_sum.at[step - 1]
        g_sum[step] = before[...] + g_in[step]

    g_copy(0, g_peers[0]).start()

    for far in (True, False):
        def start_core(k, carry, far=far):
            zz = (z + k) % depth
            for p in (0, 1):
                a, b = mine[p]
                a = 1 - a if far else a
                core_copy(p, zz, a, 1 - b).start()
                core_copy(p, zz, a, b).start()
            return carry

        lax.fori_loop(1, depth + 1, start_core, 0)

    add_gains(0)
    g_copy(1, g_peers[1]).start()

    def first_step(k, carry):
        zz = (z + k) % depth
        for far in (True, False):
            for p in (0, 1):
                a, b = mine[p]
                a = 1 - a
                b = 1 - b if far else b
                core_copy(p, zz, a, b).wait_recv()
                held = from_core.at[p, zz, a * 2 + b]
                held[...] = (wide(held) + wide(block(p, zz, a, b, c))).astype(held.dtype)
                a_copy(p, zz, a, b).start()
        return carry

    lax.fori_loop(1, depth + 1, first_step, 0)
    add_gains(1)
    g_copy(2, g_peers[2]).start()

    def chain(p, zz, b):
        a = mine[p][0]
        core_copy(p, zz, a, b).wait_recv()
        a_copy(p, zz, a, b).wait_recv()
        return (
            wide(block(p, zz, a, b, c))
            + wide(from_core.at[p, zz, a * 2 + b])
            + wide(from_first.at[p, zz, b])
        )

    def second_step(k, carry):
        zz = (z + k) % depth
        for p in (0, 1):
            b = 1 - mine[p][1]
            from_first[p, zz, b] = chain(p, zz, b).astype(from_first.dtype)
            b_copy(p, zz, b).start()
        return carry

    lax.fori_loop(1, depth + 1, second_step, 0)
    add_gains(2)

    def last_sum(p, zz):
        b = mine[p][1]
        total = chain(p, zz, b)
        b_copy(p, zz, b).wait_recv()
        return total + wide(from_second.at[p, zz])

    def third_step(k, carry):
        zz = (z + k) % depth
        for p in (0, 1):
            from_second[p, zz] = last_sum(p, zz).astype(from_second.dtype)
            z_copy(p, zz).start()
        gz_copy(zz).start()
        return carry

    lax.fori_loop(1, depth, third_step, 0)
    for p in (0, 1):
        o_ref[p] = last_sum(p, z)
    go_ref[...] = g_sum[2, z * 2 + x]

    def collect(k, carry):
        zz = (z + k) % depth
        for p in (0, 1):
            z_from(p, zz).wait_recv()
            o_ref[p] += wide(from_z.at[p, zz])
        gz_from(zz).wait_recv()
        go_ref[...] += g_z[zz]
        for p in (0, 1):
            z_copy(p, zz).wait_send()
        gz_copy(zz).wait_send()
        return carry

    lax.fori_loop(1, depth, collect, 0)

    def finish(k, carry):
        zz = (z + k) % depth
        for p in (0, 1):
            a_own, b_own = mine[p]
            for b in (0, 1):
                for a in (0, 1):
                    core_copy(p, zz, a, b).wait_send()
                a_copy(p, zz, 1 - a_own, b).wait_send()
            b_copy(p, zz, 1 - b_own).wait_send()
        return carry

    lax.fori_loop(0, depth, finish, 0)
    for step in range(3):
        g_copy(step, g_peers[step]).wait_send()


def reduce_all(packed, gains_packed):
    n = lax.axis_size("dp")
    depth, rows = n // 2, packed.shape[2]
    dma = pltpu.SemaphoreType.DMA
    low = packed.dtype
    gain_shape = gains_packed.shape[1:]
    vmem = pl.BlockSpec(memory_space=pltpu.VMEM)
    return pl.pallas_call(
        functools.partial(reduce_kernel, depth),
        out_shape=(
            jax.ShapeDtypeStruct((2, rows, WIDE), jnp.float32),
            jax.ShapeDtypeStruct(gain_shape, jnp.float32),
        ),
        in_specs=[vmem] * 2,
        out_specs=(vmem,) * 2,
        scratch_shapes=[
            pltpu.VMEM((2, depth, 4, rows, WIDE), low),
            pltpu.VMEM((2, depth, 2, rows, WIDE), low),
            pltpu.VMEM((2, depth, rows, WIDE), low),
            pltpu.VMEM((2, depth, rows, WIDE), low),
            pltpu.VMEM((3, n, *gain_shape), jnp.float32),
            pltpu.VMEM((3, n, *gain_shape), jnp.float32),
            pltpu.VMEM((depth, *gain_shape), jnp.float32),
            dma((2, depth, 4)), dma((2, depth, 4)),
            dma((2, depth, 2)), dma((2, depth, 2)),
            dma((2, depth)), dma((2, depth)), dma((2, depth)), dma((2, depth)),
            dma((3,)), dma((3,)), dma((depth,)), dma((depth,)),
        ],
        compiler_params=pltpu.CompilerParams(
            collective_id=2, has_side_effects=True, vmem_limit_bytes=40 * 2**20
        ),
    )(packed, gains_packed)


def pack_down(down, blocks, parts):
    rows = down.shape[0] // blocks
    cut = down.reshape(blocks, rows, parts, 144)
    tail = cut[..., 128:].reshape(blocks, 8, rows // 8, parts, 16)
    tail = tail.transpose(0, 2, 3, 1, 4).reshape(blocks, rows // 8, parts, 128)
    tall = jnp.concatenate([cut[..., :128], tail], axis=1)
    tall = tall.reshape(blocks, 3, -1, parts, 128).transpose(0, 2, 3, 1, 4)
    return tall.reshape(blocks, -1, parts, WIDE)


def unpack_down(held):
    blocks, short, parts, _ = held.shape
    tall = held.reshape(blocks, short, parts, 3, 128).transpose(0, 3, 1, 2, 4)
    tall = tall.reshape(blocks, 3 * short, parts, 128)
    rows = short * 8 // 3
    tail = tall[:, rows:].reshape(blocks, rows // 8, parts, 8, 16)
    tail = tail.transpose(0, 3, 1, 2, 4).reshape(blocks, rows, parts, 16)
    return jnp.concatenate([tall[:, :rows], tail], axis=-1).reshape(blocks * rows, parts * 144)


def pack(qkv, out, gate, up, down, blocks, parts):
    def cut(a):
        return a.reshape(blocks, a.shape[0] // blocks, parts, -1)

    pair = jnp.concatenate([cut(qkv), cut(out)], axis=-1)
    short = pair.shape[1]
    rows = -(-2 * short // 16) * 16
    pieces = []
    for top, bottom in ((pair, pack_down(down, blocks, parts)), (cut(gate), cut(up))):
        both = jnp.concatenate(
            [a.astype(jnp.bfloat16).reshape(blocks, short, -1) for a in (top, bottom)], axis=1
        )
        pieces.append(jnp.pad(both, ((0, 0), (0, rows - 2 * short), (0, 0))))
    return jnp.stack(pieces)


def unpack(held, short):
    _, blocks, _, width = held.shape
    parts = width // WIDE
    pair = held[0, :, :short].reshape(blocks * short, parts, WIDE)
    down = unpack_down(held[0, :, short : 2 * short].reshape(blocks, short, parts, WIDE))
    return (
        pair[..., :240].reshape(blocks * short, -1),
        pair[..., 240:].reshape(blocks * short, -1),
        held[1, :, :short].reshape(blocks * short, width),
        held[1, :, short : 2 * short].reshape(blocks * short, width),
        down,
    )


def one_hot(targets, width):
    spots = jnp.asarray(np.asarray(targets, np.int32))
    return (spots[:, None] == jnp.arange(width, dtype=jnp.int32)[None, :]).astype(jnp.bfloat16)


def picked(left, right):
    return jnp.dot(left, right, preferred_element_type=jnp.float32).astype(jnp.bfloat16)


def pair_maps(parts):
    part = np.arange(parts)[:, None]
    qkv = (part * WIDE + np.arange(240)[None, :]).reshape(-1)
    out = (part * WIDE + 240 + np.arange(144)[None, :]).reshape(-1)
    return one_hot(qkv, parts * WIDE), one_hot(out, parts * WIDE)


def down_map(parts):
    part = np.arange(parts)[:, None]
    main = (part * 144 + np.arange(128)[None, :]).reshape(-1)
    tail = (part * 144 + 128 + np.arange(16)[None, :]).reshape(-1)
    return one_hot(np.concatenate([main, tail]), parts * 144)


def tail_map(parts):
    k = np.arange(8)[:, None, None]
    part = np.arange(parts)[None, :, None]
    spots = (part * 128 + k * 16 + np.arange(16)[None, None, :]).reshape(-1)
    return one_hot(spots, parts * 128).reshape(8, parts * 16, parts * 128)


def down_from_held(held, parts):
    blocks, short, _ = held.shape
    rows = short * 8 // 3
    tall = jnp.concatenate(
        [
            jnp.concatenate(
                [held[:, :, f * WIDE + g * 128 : f * WIDE + g * 128 + 128] for f in range(parts)],
                axis=2,
            )
            for g in range(3)
        ],
        axis=1,
    )
    tail = jnp.einsum(
        "dil,kcl->dkic", tall[:, rows:], tail_map(parts), preferred_element_type=jnp.float32
    )
    tail = tail.astype(jnp.bfloat16).reshape(blocks * rows, parts * 16)
    main = tall[:, :rows].reshape(blocks * rows, parts * 128)
    return picked(jnp.concatenate([main, tail], axis=1), down_map(parts))


def down_to_held(ordered, blocks, parts):
    rows = ordered.shape[0] // blocks
    short = rows * 3 // 8
    main = ordered[:, : parts * 128].reshape(blocks, rows, parts * 128)
    tail = ordered[:, parts * 128 :].reshape(blocks, 8, rows // 8, parts * 16)
    tail = jnp.einsum(
        "dkic,kcl->dil", tail, tail_map(parts), preferred_element_type=jnp.float32
    ).astype(jnp.bfloat16)
    tall = jnp.concatenate([main, tail], axis=1)
    return jnp.concatenate(
        [
            tall[:, g * short : (g + 1) * short, f * 128 : (f + 1) * 128]
            for f in range(parts)
            for g in range(3)
        ],
        axis=2,
    )


def turned(values_in):
    half_size = values_in.shape[-1] // 2
    return jnp.concatenate([-values_in[..., half_size:], values_in[..., :half_size]], axis=-1)


def rotate(values_in, cosine, sine):
    return values_in * cosine + turned(values_in) * sine


def rotate_back(grads_in, cosine, sine):
    return grads_in * cosine - turned(grads_in * sine)


def tables(seg_ids, head_size):
    count_rows = seg_ids.shape[0]
    slot_ids = jnp.arange(count_rows, dtype=jnp.int32)
    matching = seg_ids[:, None] == seg_ids[None, :]
    first_slot = jnp.min(jnp.where(matching, slot_ids[None, :], count_rows), axis=1)
    position = (slot_ids - first_slot).astype(jnp.float32)
    frequency = rope_base ** (-jnp.arange(0, head_size, 2, dtype=jnp.float32) / head_size)
    angles = position[:, None] * frequency[None, :]
    angles = jnp.concatenate([angles, angles], axis=1)
    causal = slot_ids[None, :] <= slot_ids[:, None]
    allowed = matching & causal & (seg_ids >= 0)[None, :] | (slot_ids[None, :] == slot_ids[:, None])
    return (jnp.cos(angles), jnp.sin(angles), allowed)


def inner_rows(left, right):
    return lax.dot_general(
        left, right, (((0,), (0,)), ((), ())), preferred_element_type=jnp.float32
    )


def times_trans(left, right):
    return lax.dot_general(
        left, right, (((1,), (1,)), ((), ())), preferred_element_type=jnp.float32
    )


def per_device(tokens, seg_ids, gains, wqkv, w_out, w_gate, w_up, w_down, cotangent):
    short = wqkv.shape[0]
    blocks = lax.axis_size("dp")
    spread = jnp.pad(gains.reshape(-1), (0, 2048 - 2 * short)).reshape(16, 128)
    held, held_gains = gather_all(
        pack(wqkv, w_out, w_gate, w_up, w_down, 1, 1)[:, 0], spread
    )
    parts = lax.axis_size("fsdp")
    map_qkv, map_out = pair_maps(parts)
    pair = held[0, :, :short].reshape(blocks * short, parts * WIDE)
    full_qkv = times_trans(pair, map_qkv).astype(jnp.bfloat16)
    full_out = times_trans(pair, map_out).astype(jnp.bfloat16)
    full_gate = held[1, :, :short].reshape(blocks * short, parts * WIDE)
    full_up = held[1, :, short : 2 * short].reshape(blocks * short, parts * WIDE)
    full_down = down_from_held(held[0, :, short : 2 * short], parts)
    full_gains = held_gains.reshape(blocks, 2048)[:, : 2 * short].reshape(blocks * short, 2)
    rows_count = tokens.shape[0]
    group_size = HEADS // KV_HEADS
    width_q = HEADS * HEAD
    width_k = KV_HEADS * HEAD
    score_scale = HEAD ** (-0.5)
    cosine, sine, allowed = tables(seg_ids, HEAD)
    cos_heads = cosine[:, None, :]
    sin_heads = sine[:, None, :]
    live_rows = (seg_ids >= 0)[:, None]
    gain_one = full_gains[:, 0].astype(jnp.float32)
    gain_two = full_gains[:, 1].astype(jnp.float32)
    inputs_f = tokens.astype(jnp.float32)
    scale_one = lax.rsqrt(jnp.mean(inputs_f * inputs_f, axis=1, keepdims=True) + epsilon)
    normed = (inputs_f * scale_one * gain_one).astype(jnp.bfloat16)
    projected = jnp.dot(normed, full_qkv, preferred_element_type=jnp.float32)
    queries = rotate(
        projected[:, :width_q].reshape(rows_count, HEADS, HEAD), cos_heads, sin_heads
    ).astype(jnp.bfloat16)
    keys_low = rotate(
        projected[:, width_q : width_q + width_k].reshape(rows_count, KV_HEADS, HEAD),
        cos_heads,
        sin_heads,
    ).astype(jnp.bfloat16)
    values_low = (
        projected[:, width_q + width_k :].reshape(rows_count, KV_HEADS, HEAD).astype(jnp.bfloat16)
    )
    grouped = queries.reshape(rows_count, KV_HEADS, group_size, HEAD)
    outputs_list = []
    totals_list = []
    for head_kv in range(KV_HEADS):
        scores = (
            jnp.einsum(
                "qmd,kd->mqk",
                grouped[:, head_kv],
                keys_low[:, head_kv],
                preferred_element_type=jnp.float32,
            )
            * score_scale
        )
        scores = jnp.where(allowed[None], scores, masked_score)
        highest_score = jnp.max(scores, axis=-1, keepdims=True)
        weights_exp = jnp.exp(scores - highest_score)
        total_weight = jnp.sum(weights_exp, axis=-1, keepdims=True)
        prob_low = (weights_exp / total_weight).astype(jnp.bfloat16)
        outputs_list.append(
            jnp.einsum(
                "mqk,kd->qmd", prob_low, values_low[:, head_kv], preferred_element_type=jnp.float32
            )
        )
        totals_list.append(highest_score + jnp.log(total_weight))
    attended = jnp.stack(outputs_list, axis=1).reshape(rows_count, width_q).astype(jnp.bfloat16)
    middle = inputs_f + jnp.dot(attended, full_out, preferred_element_type=jnp.float32)
    scale_two = lax.rsqrt(jnp.mean(middle * middle, axis=1, keepdims=True) + epsilon)
    normed_two = (middle * scale_two * gain_two).astype(jnp.bfloat16)
    gate_pre = jnp.dot(normed_two, full_gate, preferred_element_type=jnp.float32)
    up_pre = jnp.dot(normed_two, full_up, preferred_element_type=jnp.float32)
    sigmoid_gate = jax.nn.sigmoid(gate_pre)
    activated = gate_pre * sigmoid_gate
    hidden = (activated * up_pre).astype(jnp.bfloat16)
    result = middle + jnp.dot(hidden, full_down, preferred_element_type=jnp.float32)
    out_tokens = jnp.where(live_rows, result, 0.0).astype(jnp.bfloat16)
    grad_out = jnp.where(live_rows, cotangent, jnp.zeros_like(cotangent))
    grad_out_ordered = times_trans(grad_out, down_map(parts)).astype(jnp.bfloat16)
    grad_down = inner_rows(hidden, grad_out_ordered).astype(jnp.bfloat16)
    held_down = down_to_held(grad_down, blocks, parts)
    grad_hidden = times_trans(grad_out, full_down)
    grad_gate_pre = (
        grad_hidden * up_pre * sigmoid_gate * (1.0 + gate_pre * (1.0 - sigmoid_gate))
    ).astype(jnp.bfloat16)
    grad_up_pre = (grad_hidden * activated).astype(jnp.bfloat16)
    grad_gate = inner_rows(normed_two, grad_gate_pre)
    grad_up = inner_rows(normed_two, grad_up_pre)
    grad_normed_two = times_trans(grad_gate_pre, full_gate) + times_trans(grad_up_pre, full_up)
    grad_gain_two = jnp.sum(grad_normed_two * middle * scale_two, axis=0)
    weighted_two = grad_normed_two * gain_two
    grad_middle = (
        grad_out.astype(jnp.float32)
        + scale_two * weighted_two
        - middle * scale_two**3 * jnp.mean(weighted_two * middle, axis=1, keepdims=True)
    )
    grad_branch = grad_middle.astype(jnp.bfloat16)
    grad_attended = (
        times_trans(grad_branch, full_out)
        .astype(jnp.bfloat16)
        .reshape(rows_count, KV_HEADS, group_size, HEAD)
    )
    query_grads = []
    key_grads = []
    value_grads = []
    for head_kv in range(KV_HEADS):
        query_part = grouped[:, head_kv]
        key_part = keys_low[:, head_kv]
        value_part = values_low[:, head_kv]
        grad_part = grad_attended[:, head_kv]
        scores = (
            jnp.einsum("qmd,kd->mqk", query_part, key_part, preferred_element_type=jnp.float32)
            * score_scale
        )
        scores = jnp.where(allowed[None], scores, masked_score)
        probs_full = jnp.exp(scores - totals_list[head_kv])
        prob_low = probs_full.astype(jnp.bfloat16)
        value_grads.append(
            jnp.einsum("mqk,qmd->kd", prob_low, grad_part, preferred_element_type=jnp.float32)
        )
        grad_prob = jnp.einsum(
            "qmd,kd->mqk", grad_part, value_part, preferred_element_type=jnp.float32
        )
        row_delta = jnp.sum(grad_prob * probs_full, axis=-1, keepdims=True)
        grad_scores = (probs_full * (grad_prob - row_delta)).astype(jnp.bfloat16)
        query_grads.append(
            jnp.einsum("mqk,kd->qmd", grad_scores, key_part, preferred_element_type=jnp.float32)
            * score_scale
        )
        key_grads.append(
            jnp.einsum("mqk,qmd->kd", grad_scores, query_part, preferred_element_type=jnp.float32)
            * score_scale
        )
    grad_queries = rotate_back(
        jnp.stack(query_grads, axis=1).reshape(rows_count, HEADS, HEAD), cos_heads, sin_heads
    )
    grad_keys = rotate_back(jnp.stack(key_grads, axis=1), cos_heads, sin_heads)
    grad_values = jnp.stack(value_grads, axis=1)
    grad_projected = jnp.concatenate(
        [
            grad_queries.reshape(rows_count, width_q),
            grad_keys.reshape(rows_count, width_k),
            grad_values.reshape(rows_count, width_k),
        ],
        axis=1,
    ).astype(jnp.bfloat16)
    grad_pair = inner_rows(normed, picked(grad_projected, map_qkv)) + inner_rows(
        attended, picked(grad_branch, map_out)
    )
    grad_normed = times_trans(grad_projected, full_qkv)
    grad_gain_one = jnp.sum(grad_normed * inputs_f * scale_one, axis=0)
    weighted_one = grad_normed * gain_one
    grad_inputs = (
        grad_middle
        + scale_one * weighted_one
        - inputs_f * scale_one**3 * jnp.mean(weighted_one * inputs_f, axis=1, keepdims=True)
    )
    grad_tokens = grad_inputs.astype(jnp.bfloat16)
    grad_gains = jnp.stack([grad_gain_one, grad_gain_two], axis=1)
    def blocked(a):
        return a.astype(jnp.bfloat16).reshape(blocks, short, parts * WIDE)

    rest = held.shape[2] - 2 * short
    packed = jnp.stack(
        [
            jnp.concatenate([blocked(grad_pair), held_down], axis=1),
            jnp.concatenate([blocked(grad_gate), blocked(grad_up)], axis=1),
        ]
    )
    packed = jnp.pad(packed, ((0, 0), (0, 0), (0, rest), (0, 0)))
    flat_gains = jnp.pad(grad_gains.reshape(blocks, -1), ((0, 0), (0, 1024 - 2 * short)))
    owned, owned_gains = reduce_all(packed, flat_gains.reshape(blocks, 8, 128))
    own_qkv, own_out, own_gate, own_up, own_down = unpack(owned[:, None], short)
    own_gains = owned_gains.reshape(-1)[: 2 * short].reshape(short, 2)
    return (out_tokens, grad_tokens, own_gains, own_qkv, own_out, own_gate, own_up, own_down)


def solution(mesh):
    placed = (
        P(("dp", "fsdp"), None),
        P(("dp", "fsdp")),
        P("dp", None),
        P("dp", "fsdp"),
        P("dp", "fsdp"),
        P("dp", "fsdp"),
        P("dp", "fsdp"),
        P("dp", "fsdp"),
        P(("dp", "fsdp"), None),
    )
    return jax.shard_map(
        per_device,
        mesh=mesh,
        in_specs=placed,
        out_specs=(
            P(("dp", "fsdp"), None),
            P(("dp", "fsdp"), None),
            P("dp", None),
            P("dp", "fsdp"),
            P("dp", "fsdp"),
            P("dp", "fsdp"),
            P("dp", "fsdp"),
            P("dp", "fsdp"),
        ),
        check_vma=False,
    )
```
